128 devices in a mesh: layer: 8 (over x_lo, z), example: 16 (over x_hi, y, core).
Axes of the slice: x: 4 (x_hi: 2, x_lo: 2; x = x_hi * 2 + x_lo), y: 4, z: 4, core: 2. Of those that a mesh axis runs over, the one named last changes fastest.
Arguments:
- queries: float32 [8, 256, 1024], P('layer', 'example'), may hold values from -0.0625 to 0.0625
- precond: float32 [8, 1024, 1024], P('layer', 'example'), may hold values from -7 to 7.5, as said below
- store: float32 [8, 65536, 1024], P('layer', 'example'), may hold values from -2000 to 2000
Outputs:
- influence: float32 [256, 65536], P('layer', 'example')
The draws below stay inside these ranges and needn't reach their ends.
Inputs may be any that keep to these rules, and one draw needn't show every extreme that they name: `precond`: each layer's preconditioner is symmetric positive definite, a damped Gram matrix with every eigenvalue at least 0.25.
All inputs are finite; a program needn't handle non-finite values.
Results may differ from the reference program's by a relative error of at most 0.0001.
Values sent between devices are 32-bit elements; how exact they have to be, the bound alone decides.
No kernel may reach another device: no remote copies, remote signals or barrier semaphores. Data moves between devices by JAX's collectives and lax.ppermute only.
A program may use at most 128 MiB of HBM per device.

```python
import math
import jax
import jax.numpy as jnp
from jax import lax

R = 1024
Q = 256
LAYERS = 8
EXAMPLES = 65536


def gram_factors(key):
    key = jax.random.fold_in(key, 5)
    key_mat, key_cols = jax.random.split(key)
    lead_count = min(16, R // 4)
    entries = jax.random.uniform(key_mat, (LAYERS, R, R), jnp.float32, -math.sqrt(3.0), math.sqrt(3.0))
    col_pos = jax.random.uniform(key_cols, (LAYERS, 1, R), jnp.float32, 0.0, 1.0)
    scales = jnp.exp(math.log(0.25) + col_pos * math.log(6.0))
    leading = jnp.arange(R)[None, None, :] < lead_count
    scales = jnp.where(leading, 1.5, scales)
    return (entries * scales, lead_count)


def draw_precond(key, part):
    factors, lead_count = gram_factors(key)
    damping = 0.5
    gram = jnp.einsum('lik,ljk->lij', factors, factors, precision=lax.Precision.HIGHEST) * (1.0 / R)
    gram = 0.5 * (gram + jnp.swapaxes(gram, 1, 2))
    eye_mat = jnp.eye(R, dtype=jnp.float32)[None, :, :]
    return gram + damping * eye_mat


def draw_store(key, part):
    factors, lead_count = gram_factors(key)
    key = jax.random.fold_in(key, 23)
    key_base = jax.random.fold_in(key, 0)
    key_rows = jax.random.fold_in(key, 1)
    key_coef = jax.random.fold_in(key, 3)
    shape = (LAYERS, EXAMPLES, R)
    layer_pos = jnp.arange(LAYERS, dtype=jnp.float32) / max(LAYERS - 1, 1)
    layer_factor = jnp.exp(layer_pos * math.log(3.0))[:, None, None]
    directions = factors[:, :, :lead_count]
    coefs = jax.random.normal(key_coef, (LAYERS, EXAMPLES, lead_count), jnp.float32) * (1.0 / (1.5 * math.sqrt(lead_count)))
    aligned = jnp.einsum('lek,lrk->ler', coefs, directions, precision=lax.Precision.HIGHEST)
    base = jax.random.normal(key_base, shape, jnp.float32)
    row_scale = jnp.exp(jax.random.uniform(key_rows, (LAYERS, EXAMPLES, 1), jnp.float32, 0.0, math.log(10.0)))
    return (base + aligned) * row_scale * layer_factor


def steps_of(key, dims, cuts, smallest, top_value):
    def one(axis_at, blocks):
        heights = jax.random.uniform(jax.random.fold_in(jax.random.fold_in(key, 6), axis_at), (blocks,), jnp.float32, smallest / len(cuts), top_value / len(cuts))
        return jnp.repeat(jnp.exp(heights), dims[axis_at] // blocks).reshape((-1,) + (1,) * (len(dims) - axis_at - 1))

    loudness = one(*cuts[0])
    for cut in cuts[1:]:
        loudness = loudness * one(*cut)
    return loudness


def centred(key, extent, width, most, shards=(), kind=jnp.bfloat16):
    gain = steps_of(key, extent, shards, -0.22, 0.18) if shards else 1.0
    values = jax.random.normal(key, extent, jnp.float32) * width * gain
    return jnp.minimum(jnp.maximum(values, -most), most).astype(kind)


def setup_inputs(seed: int = 0) -> dict:
    seeds = jax.random.split(jax.random.key(seed), 4)
    queries = centred(seeds[0], (LAYERS, Q, R), (R * LAYERS) ** -0.5, 0.0625, ((0, 8), (1, 16)), jnp.float32)
    precond = draw_precond(jax.random.fold_in(seeds[3], 71), 0)
    store = draw_store(jax.random.fold_in(seeds[3], 71), 0)
    return {"queries": queries, "precond": precond, "store": store}


def reference(queries, precond, store):

    def layer_step(carry, inputs):
        scores, sizes_sq = carry
        query_rows, matrix, grads = inputs
        ready = jnp.dot(query_rows, matrix, precision=lax.Precision.HIGHEST, preferred_element_type=jnp.float32)
        moved = jnp.dot(grads, matrix, precision=lax.Precision.HIGHEST, preferred_element_type=jnp.float32)
        sizes_sq = sizes_sq + lax.optimization_barrier(jnp.sum(moved * grads, axis=1))
        scores = scores + jnp.dot(ready, grads.T, precision=lax.Precision.HIGHEST, preferred_element_type=jnp.float32)
        return ((scores, sizes_sq), None)
    start = (jnp.zeros((Q, EXAMPLES), jnp.float32), jnp.zeros((EXAMPLES,), jnp.float32))
    (scores, sizes_sq), unused = lax.scan(layer_step, start, (queries, precond, store))
    return scores / jnp.sqrt(sizes_sq)[None, :]
```

```python
import functools

import jax
import jax.numpy as jnp
from jax import lax
from jax.experimental import pallas as pl
from jax.experimental.pallas import tpu as pltpu
from jax.sharding import PartitionSpec as P

R = 1024
Q = 256
ROWS = 64
QROWS = 16
PIECE = ROWS + QROWS
TILE = 1024
SPLIT = (2048, 2048)
BF16 = jnp.bfloat16
F32 = jnp.float32
LIMIT = 20 * 2**20
nt_dot = functools.partial(
    lax.dot_general, dimension_numbers=(((1,), (1,)), ((), ())), preferred_element_type=F32
)
VMEM = pl.BlockSpec(memory_space=pltpu.VMEM)
SMEM = pl.BlockSpec(memory_space=pltpu.SMEM)


def example_permute(x, to):
    pairs = []
    for x_hi in range(2):
        for y in range(4):
            for core in range(2):
                a, b, c = to(x_hi, y, core)
                pairs.append((x_hi * 8 + y * 2 + core, a * 8 + (b % 4) * 2 + c))
    return lax.ppermute(x, "example", pairs)


def layer_permute(x, to):
    pairs = []
    for x_lo in range(2):
        for z in range(4):
            a, b = to(x_lo, z)
            pairs.append((x_lo * 4 + z, a * 4 + b % 4))
    return lax.ppermute(x, "layer", pairs)


def swap_core(x):
    return example_permute(x, lambda x_hi, y, core: (x_hi, y, 1 - core))


def z_up(x):
    return layer_permute(x, lambda x_lo, z: (x_lo, z + 1))


def z_down(x):
    return layer_permute(x, lambda x_lo, z: (x_lo, z - 1))


def swap_x(x):
    return layer_permute(x, lambda x_lo, z: (1 - x_lo, z))


NEAR = [(0, 0, 0, 0), (0, PIECE, 1, 0), (1, 0, 0, 1), (1, PIECE, 1, 1)]
FAR = [(0, 0, 0, 0), (1, 0, 1, 0), (2, 0, 0, 1), (3, 0, 1, 1)]


def tie(*arrays):
    return lax.optimization_barrier(arrays)


def split(blocks, bufs, x_hi, core, hi_ref, lo_ref):
    for b, off, x_flip, core_flip in blocks:
        at = ((x_hi + x_flip) % 2) * 2 + (core + core_flip) % 2
        rows = pl.ds(pl.multiple_of(at * ROWS, ROWS), ROWS)
        block = bufs[b][off : off + ROWS, :]
        hi = block.astype(BF16)
        hi_ref[rows, :] = hi
        lo_ref[rows, :] = (block - hi.astype(F32)).astype(BF16)


def add_sizes(y_shifts, y, s_ref, matrices, o_ref):
    @pl.loop(0, o_ref.shape[1] // TILE)
    def _(i):
        rows = pl.ds(pl.multiple_of(i * TILE, TILE), TILE)
        sh = s_ref[rows, :].astype(BF16)
        total = 0.0
        for y_shift, (hi_ref, lo_ref) in zip(y_shifts, matrices):
            moved = nt_dot(sh, hi_ref[...]) + nt_dot(sh, lo_ref[...])
            first = pl.multiple_of(((y + y_shift + 4) % 4) * 128, 128)
            for half in range(2):
                cols = pl.ds(first + half * 512, 128)
                own = s_ref[rows, cols]
                weight = 2.0 * own - own.astype(BF16).astype(F32)
                total += moved[:, half * 128 : half * 128 + 128] * weight
        o_ref[:, rows] = jnp.sum(total.T, axis=0, keepdims=True)


def part_kernel(blocks, y_shift, n, where_ref, *refs):
    bufs, (s_ref, hi_ref, lo_ref, o_ref) = refs[:n], refs[n:]
    me = where_ref[0]
    split(blocks, bufs, me // 8, me % 2, hi_ref, lo_ref)
    add_sizes([y_shift], (me // 2) % 4, s_ref, [(hi_ref, lo_ref)], o_ref)


def part_sizes(where, part, store):
    y_shift, buffers, blocks = part
    examples = store.shape[0]
    return pl.pallas_call(
        functools.partial(part_kernel, blocks, y_shift, len(buffers)),
        in_specs=[SMEM] + [VMEM] * (len(buffers) + 1),
        out_specs=[VMEM] * 3,
        out_shape=[jax.ShapeDtypeStruct((256, R), BF16)] * 2 + [jax.ShapeDtypeStruct((1, examples), F32)],
        compiler_params=pltpu.CompilerParams(vmem_limit_bytes=LIMIT),
        cost_estimate=pl.CostEstimate(
            flops=8 * 256 * R * examples, bytes_accessed=4 * R * examples, transcendentals=0
        ),
    )(where, *buffers, store)


def rest_kernel(y_shifts, where_ref, *refs):
    mats, (s_ref, o_ref) = refs[:-2], refs[-2:]
    pairs = [(mats[2 * k], mats[2 * k + 1]) for k in range(len(y_shifts))]
    add_sizes(y_shifts, (where_ref[0] // 2) % 4, s_ref, pairs, o_ref)


def rest_sizes(where, y_shifts, matrices, store):
    examples = store.shape[0]
    return pl.pallas_call(
        functools.partial(rest_kernel, y_shifts),
        in_specs=[SMEM] + [VMEM] * (len(matrices) + 1),
        out_specs=VMEM,
        out_shape=jax.ShapeDtypeStruct((1, examples), F32),
        compiler_params=pltpu.CompilerParams(vmem_limit_bytes=LIMIT),
        cost_estimate=pl.CostEstimate(
            flops=8 * 256 * len(y_shifts) * R * examples, bytes_accessed=4 * R * examples, transcendentals=0
        ),
    )(where, *matrices, store)


SLOTS = (6, 7, 4, 1, 0, 2, 3, 5)


def ready_kernel(parts, n, where_ref, *refs):
    ins, (rh_ref, rl_ref, *made), q_ref = refs[:n], refs[n:-1], refs[-1]
    me, x_lo, z = where_ref[0], where_ref[1], where_ref[2]
    x_hi, y, core = me // 8, (me // 2) % 4, me % 2
    matrices = []
    for y_shift, first, count, blocks, ready_made in parts:
        bufs = ins[first : first + count]
        if ready_made:
            matrices.append((y_shift, ins[first + count], ins[first + count + 1]))
        else:
            hi_ref, lo_ref, *made = made
            split(blocks, bufs, x_hi, core, hi_ref, lo_ref)
            matrices.append((y_shift, hi_ref, lo_ref))
        for b, off, x_flip, core_flip in blocks:
            to_z, to_x = (y + y_shift + 4) % 4, (x_hi + x_flip) % 2
            code = ((to_z - z + 4) % 4) * 2 + (to_x + x_lo) % 2
            slot = sum(jnp.where(code == k, s, 0) for k, s in enumerate(SLOTS))
            at = slot * 2 + (core + core_flip) % 2
            rows = pl.ds(pl.multiple_of(at * QROWS, QROWS), QROWS)
            q_ref[rows, :] = bufs[b][off + ROWS : off + PIECE, :]
    q = q_ref[...]
    qh = q.astype(BF16)
    ql = (q - qh.astype(F32)).astype(BF16)
    for y_shift, hi_ref, lo_ref in matrices:
        ready = nt_dot(qh, hi_ref[...]) + nt_dot(qh, lo_ref[...]) + nt_dot(ql, hi_ref[...])
        high = ready.astype(BF16)
        low = (ready - high.astype(F32)).astype(BF16)
        start = pl.multiple_of(((y + y_shift + 4) % 4) * 128, 128)
        for half in range(2):
            cols = pl.ds(start + half * 512, 128)
            rh_ref[:, cols] = high[:, half * 128 : half * 128 + 128]
            rl_ref[:, cols] = low[:, half * 128 : half * 128 + 128]


def ready_queries(where, parts, matrices):
    refs, rows, missing = [], [], 0
    for (y_shift, buffers, blocks), made in zip(parts, matrices):
        rows.append((y_shift, len(refs), len(buffers), blocks, bool(made)))
        refs += list(buffers) + list(made)
        missing += not made
    shapes = [(Q, R)] * 2 + [(256, R)] * (2 * missing)
    return pl.pallas_call(
        functools.partial(ready_kernel, rows, len(refs)),
        in_specs=[SMEM] + [VMEM] * len(refs),
        out_specs=[VMEM] * len(shapes),
        out_shape=[jax.ShapeDtypeStruct(shape, BF16) for shape in shapes],
        scratch_shapes=[pltpu.VMEM((Q, R), F32)],
        compiler_params=pltpu.CompilerParams(vmem_limit_bytes=LIMIT),
        cost_estimate=pl.CostEstimate(flops=6 * Q * R * R, bytes_accessed=2**20, transcendentals=0),
    )(where, *refs)


CUTS = (64, 64, 32, 32, 64)


def raw_kernel(first, rh_ref, rl_ref, s_ref, *outs):
    @pl.loop(0, outs[0].shape[1] // TILE)
    def _(i):
        rows = pl.ds(pl.multiple_of(first + i * TILE, TILE), TILE)
        cols = pl.ds(pl.multiple_of(i * TILE, TILE), TILE)
        s = s_ref[rows, :]
        sh = s.astype(BF16)
        sl = (s - sh.astype(F32)).astype(BF16)
        raw = nt_dot(rh_ref[...], sh) + nt_dot(rh_ref[...], sl) + nt_dot(rl_ref[...], sh)
        at = 0
        for n, ref in zip(CUTS, outs):
            ref[:, cols] = raw[at : at + n]
            at += n


def raw_scores(rh, rl, store, first, examples):
    return pl.pallas_call(
        functools.partial(raw_kernel, first),
        in_specs=[VMEM] * 3,
        out_specs=[VMEM] * len(CUTS),
        out_shape=[jax.ShapeDtypeStruct((n, examples), F32) for n in CUTS],
        compiler_params=pltpu.CompilerParams(vmem_limit_bytes=LIMIT),
        cost_estimate=pl.CostEstimate(
            flops=8 * Q * R * examples, bytes_accessed=4 * (R + Q) * examples, transcendentals=0
        ),
    )(rh, rl, store)


def shards(queries, precond, store):
    layer = lax.axis_index("layer")
    where = jnp.stack([lax.axis_index("example"), layer // 4, layer % 4]).astype(jnp.int32)
    store = store[0]

    piece = jnp.concatenate([precond[0], queries[0]], axis=0)
    other = example_permute(piece, lambda x_hi, y, core: (1 - x_hi, y, core))
    pair = jnp.concatenate([piece, other], axis=0)
    left = example_permute(pair, lambda x_hi, y, core: (x_hi, y + 1, core))
    right = example_permute(pair, lambda x_hi, y, core: (x_hi, y - 1, core))
    own = (0, [pair, swap_core(pair)], NEAR)
    own_hi, own_lo, own_part = part_sizes(where, own, store)
    left, right, own_part = tie(left, right, own_part)
    far0 = example_permute(left[:PIECE], lambda x_hi, y, core: (x_hi, y + 1, core))
    far1 = example_permute(right[PIECE:], lambda x_hi, y, core: (x_hi, y - 1, core))
    below = (-1, [left, swap_core(left)], NEAR)
    below_hi, below_lo, below_part = part_sizes(where, below, store)
    above = (1, [right, swap_core(right)], NEAR)
    far0, far1, below_part = tie(far0, far1, below_part)
    across = (2, [far0, far1, swap_core(far0), swap_core(far1)], FAR)
    rh, rl, *rest = ready_queries(
        where, [own, below, above, across], [(own_hi, own_lo), (below_hi, below_lo), (), ()]
    )

    blocks, first = [], 0
    for examples in SPLIT:
        blocks.append(raw_scores(rh, rl, store, first, examples))
        rh = tie(rh, blocks[-1][-1])[0]
        first += examples
    (up1, down1, up2, down2, mine), (up1b, down1b, up2b, down2b, mineb) = blocks
    from_below, from_above = z_up(up1), z_down(down1)
    from_belowb, from_aboveb = z_up(up1b), z_down(down1b)
    *rest, from_below, from_above = tie(*rest, from_below, from_above)
    rest_part = rest_sizes(where, [1, 2], rest, store)
    last_below, last_above = z_up(up2 + from_below[:32]), z_down(down2 + from_above[:32])
    here = mine[:32] + from_above[32:] + last_below
    there = mine[32:] + from_below[32:] + last_above
    scores = [here + swap_x(there)]
    sizes_sq = own_part + below_part + rest_part
    sizes_sq, from_belowb, from_aboveb = tie(sizes_sq, from_belowb, from_aboveb)
    last_below, last_above = z_up(up2b + from_belowb[:32]), z_down(down2b + from_aboveb[:32])
    here = mineb[:32] + from_aboveb[32:] + last_below
    there = mineb[32:] + from_belowb[32:] + last_above
    scores.append(here + swap_x(there))

    sizes_sq = sizes_sq + z_up(sizes_sq) + z_down(sizes_sq) + layer_permute(sizes_sq, lambda x, z: (x, z + 2))
    root = jnp.sqrt(sizes_sq + swap_x(sizes_sq))
    return jnp.concatenate(scores, axis=1) / root


def solution(mesh):
    in_specs = (
        P("layer", "example", None),
        P("layer", "example", None),
        P("layer", "example", None),
    )
    out_specs = P("layer", "example")
    return jax.shard_map(shards, mesh=mesh, in_specs=in_specs, out_specs=out_specs, check_vma=False)
```

```python
import functools

import jax
import jax.numpy as jnp
from jax import lax
from jax.experimental import pallas as pl
from jax.experimental.pallas import tpu as pltpu
from jax.sharding import PartitionSpec as P

R = 1024
Q = 256
ROWS = 64
QROWS = 16
PIECE = ROWS + QROWS
TILE = 1024
RAW_TILE = 512
SPLIT = (2560, 1536)
BF16 = jnp.bfloat16
F32 = jnp.float32
LIMIT = 20 * 2**20
nt_dot = functools.partial(
    lax.dot_general, dimension_numbers=(((1,), (1,)), ((), ())), preferred_element_type=F32
)
VMEM = pl.BlockSpec(memory_space=pltpu.VMEM)
SMEM = pl.BlockSpec(memory_space=pltpu.SMEM)


def example_permute(x, to):
    pairs = []
    for x_hi in range(2):
        for y in range(4):
            for core in range(2):
                a, b, c = to(x_hi, y, core)
                pairs.append((x_hi * 8 + y * 2 + core, a * 8 + (b % 4) * 2 + c))
    return lax.ppermute(x, "example", pairs)


def layer_permute(x, to):
    pairs = []
    for x_lo in range(2):
        for z in range(4):
            a, b = to(x_lo, z)
            pairs.append((x_lo * 4 + z, a * 4 + b % 4))
    return lax.ppermute(x, "layer", pairs)


def y_up(x):
    return example_permute(x, lambda x_hi, y, core: (x_hi, y + 1, core))


def y_down(x):
    return example_permute(x, lambda x_hi, y, core: (x_hi, y - 1, core))


def with_swapped(*arrays):
    return list(arrays) + [example_permute(x, lambda x_hi, y, core: (x_hi, y, 1 - core)) for x in arrays]


def z_up(x):
    return layer_permute(x, lambda x_lo, z: (x_lo, z + 1))


def z_down(x):
    return layer_permute(x, lambda x_lo, z: (x_lo, z - 1))


def swap_x(x):
    return layer_permute(x, lambda x_lo, z: (1 - x_lo, z))


HEAD = 32
NEAR = [(0, 0, ROWS, ROWS, 0, 0), (1, 0, ROWS, ROWS, 1, 0), (2, 0, ROWS, ROWS, 0, 1), (3, 0, ROWS, ROWS, 1, 1)]
FAR = [
    (4 * core + 2 * x_flip + tail, HEAD * tail, HEAD, HEAD if tail else -1, x_flip, core)
    for core in range(2)
    for x_flip in range(2)
    for tail in range(2)
]


def tie(*arrays):
    return lax.optimization_barrier(arrays)


def split(blocks, bufs, x_hi, core, hi_ref, lo_ref):
    for b, first, n, _, x_flip, core_flip in blocks:
        at = ((x_hi + x_flip) % 2) * 2 + (core + core_flip) % 2
        rows = pl.ds(pl.multiple_of(at * ROWS + first, HEAD), n)
        block = bufs[b][:n, :]
        hi = block.astype(BF16)
        hi_ref[rows, :] = hi
        lo_ref[rows, :] = (block - hi.astype(F32)).astype(BF16)


def add_sizes(y_shifts, y, s_ref, matrices, o_ref):
    @pl.loop(0, o_ref.shape[1] // TILE)
    def _(i):
        rows = pl.ds(pl.multiple_of(i * TILE, TILE), TILE)
        sh = s_ref[rows, :].astype(BF16)
        total = 0.0
        for y_shift, (hi_ref, lo_ref) in zip(y_shifts, matrices):
            moved = nt_dot(sh, hi_ref[...]) + nt_dot(sh, lo_ref[...])
            first = pl.multiple_of(((y + y_shift + 4) % 4) * 128, 128)
            for half in range(2):
                cols = pl.ds(first + half * 512, 128)
                own = s_ref[rows, cols]
                weight = 2.0 * own - own.astype(BF16).astype(F32)
                total += moved[:, half * 128 : half * 128 + 128] * weight
        o_ref[:, rows] = jnp.sum(total.T, axis=0, keepdims=True)


def part_kernel(blocks, y_shift, n, where_ref, *refs):
    bufs, (s_ref, hi_ref, lo_ref, o_ref) = refs[:n], refs[n:]
    me = where_ref[0]
    split(blocks, bufs, me // 8, me % 2, hi_ref, lo_ref)
    add_sizes([y_shift], (me // 2) % 4, s_ref, [(hi_ref, lo_ref)], o_ref)


def part_sizes(where, part, store):
    y_shift, buffers, blocks = part
    examples = store.shape[0]
    return pl.pallas_call(
        functools.partial(part_kernel, blocks, y_shift, len(buffers)),
        in_specs=[SMEM] + [VMEM] * (len(buffers) + 1),
        out_specs=[VMEM] * 3,
        out_shape=[jax.ShapeDtypeStruct((256, R), BF16)] * 2 + [jax.ShapeDtypeStruct((1, examples), F32)],
        compiler_params=pltpu.CompilerParams(vmem_limit_bytes=LIMIT),
        cost_estimate=pl.CostEstimate(
            flops=8 * 256 * R * examples, bytes_accessed=4 * R * examples, transcendentals=0
        ),
    )(where, *buffers, store)


def rest_kernel(y_shifts, where_ref, *refs):
    mats, (s_ref, o_ref) = refs[:-2], refs[-2:]
    pairs = [(mats[2 * k], mats[2 * k + 1]) for k in range(len(y_shifts))]
    add_sizes(y_shifts, (where_ref[0] // 2) % 4, s_ref, pairs, o_ref)


def rest_sizes(where, y_shifts, matrices, store):
    examples = store.shape[0]
    return pl.pallas_call(
        functools.partial(rest_kernel, y_shifts),
        in_specs=[SMEM] + [VMEM] * (len(matrices) + 1),
        out_specs=VMEM,
        out_shape=jax.ShapeDtypeStruct((1, examples), F32),
        compiler_params=pltpu.CompilerParams(vmem_limit_bytes=LIMIT),
        cost_estimate=pl.CostEstimate(flops=1, bytes_accessed=1, transcendentals=0),
    )(where, *matrices, store)


SLOTS = (6, 7, 4, 1, 0, 2, 3, 5)


def ready_kernel(parts, n, where_ref, *refs):
    ins, (rh_ref, rl_ref, *made), q_ref = refs[:n], refs[n:-1], refs[-1]
    me, x_lo, z = where_ref[0], where_ref[1], where_ref[2]
    x_hi, y, core = me // 8, (me // 2) % 4, me % 2
    matrices = []
    for y_shift, first, count, blocks, ready_made in parts:
        bufs = ins[first : first + count]
        if ready_made:
            matrices.append((y_shift, ins[first + count], ins[first + count + 1]))
        else:
            hi_ref, lo_ref, *made = made
            split(blocks, bufs, x_hi, core, hi_ref, lo_ref)
            matrices.append((y_shift, hi_ref, lo_ref))
        for b, _, _, queries, x_flip, core_flip in blocks:
            if queries < 0:
                continue
            to_z, to_x = (y + y_shift + 4) % 4, (x_hi + x_flip) % 2
            code = ((to_z - z + 4) % 4) * 2 + (to_x + x_lo) % 2
            slot = sum(jnp.where(code == k, s, 0) for k, s in enumerate(SLOTS))
            at = slot * 2 + (core + core_flip) % 2
            rows = pl.ds(pl.multiple_of(at * QROWS, QROWS), QROWS)
            q_ref[rows, :] = bufs[b][queries : queries + QROWS, :]
    q = q_ref[...]
    qh = q.astype(BF16)
    ql = (q - qh.astype(F32)).astype(BF16)
    for y_shift, hi_ref, lo_ref in matrices:
        ready = nt_dot(qh, hi_ref[...]) + nt_dot(qh, lo_ref[...]) + nt_dot(ql, hi_ref[...])
        high = ready.astype(BF16)
        low = (ready - high.astype(F32)).astype(BF16)
        start = pl.multiple_of(((y + y_shift + 4) % 4) * 128, 128)
        for half in range(2):
            cols = pl.ds(start + half * 512, 128)
            rh_ref[:, cols] = high[:, half * 128 : half * 128 + 128]
            rl_ref[:, cols] = low[:, half * 128 : half * 128 + 128]


def ready_queries(where, parts, matrices):
    refs, rows, missing = [], [], 0
    for (y_shift, buffers, blocks), made in zip(parts, matrices):
        rows.append((y_shift, len(refs), len(buffers), blocks, bool(made)))
        refs += list(buffers) + list(made)
        missing += not made
    shapes = [(Q, R)] * 2 + [(256, R)] * (2 * missing)
    return pl.pallas_call(
        functools.partial(ready_kernel, rows, len(refs)),
        in_specs=[SMEM] + [VMEM] * len(refs),
        out_specs=[VMEM] * len(shapes),
        out_shape=[jax.ShapeDtypeStruct(shape, BF16) for shape in shapes],
        scratch_shapes=[pltpu.VMEM((Q, R), F32)],
        compiler_params=pltpu.CompilerParams(vmem_limit_bytes=LIMIT),
        cost_estimate=pl.CostEstimate(flops=6 * Q * R * R, bytes_accessed=2**20, transcendentals=0),
    )(where, *refs)


Z_FIRST = [[(0, 64)], [(64, 64)], [(128, 32)], [(160, 32)], [(192, 64)]]
HALVES = ((2, 0), (1, 1), (2, 1), (3, 0), (1, 0), (3, 1), (0, 0), (0, 1))
X_FIRST = [[(32 * SLOTS[2 * dz + dx] + 16 * half, 16) for dz, half in HALVES] for dx in (1, 0)]


def raw_kernel(first, runs, rh_ref, rl_ref, s_ref, *outs):
    @pl.loop(0, outs[0].shape[1] // RAW_TILE)
    def _(i):
        rows = pl.ds(pl.multiple_of(first + i * RAW_TILE, RAW_TILE), RAW_TILE)
        cols = pl.ds(pl.multiple_of(i * RAW_TILE, RAW_TILE), RAW_TILE)
        s = s_ref[rows, :]
        sh = s.astype(BF16)
        sl = (s - sh.astype(F32)).astype(BF16)
        raw = nt_dot(rh_ref[...], sh) + nt_dot(rh_ref[...], sl) + nt_dot(rl_ref[...], sh)
        for run, ref in zip(runs, outs):
            at = 0
            for start, n in run:
                ref[at : at + n, cols] = raw[start : start + n]
                at += n


def raw_scores(rh, rl, store, first, examples, runs):
    return pl.pallas_call(
        functools.partial(raw_kernel, first, runs),
        in_specs=[VMEM] * 3,
        out_specs=[VMEM] * len(runs),
        out_shape=[jax.ShapeDtypeStruct((sum(n for _, n in run), examples), F32) for run in runs],
        compiler_params=pltpu.CompilerParams(vmem_limit_bytes=LIMIT),
        cost_estimate=pl.CostEstimate(
            flops=8 * Q * R * examples, bytes_accessed=4 * (R + Q) * examples, transcendentals=0
        ),
    )(rh, rl, store)


def shards(queries, precond, store):
    layer = lax.axis_index("layer")
    where = jnp.stack([lax.axis_index("example"), layer // 4, layer % 4]).astype(jnp.int32)
    store = store[0]

    own0 = jnp.concatenate([precond[0], queries[0]], axis=0)
    own1 = example_permute(own0, lambda x_hi, y, core: (1 - x_hi, y, core))
    own1, below0, above0 = tie(own1, y_up(own0), y_down(own0))
    own = (0, with_swapped(own0, own1), NEAR)
    own_hi, own_lo, own_part = part_sizes(where, own, store)
    below1, above1, *far0, own_part = tie(
        y_up(own1), y_down(own1), y_up(below0[:HEAD]), y_down(above0[HEAD:]), own_part
    )
    tail, head = y_up(below1[HEAD:]), y_down(above1[:HEAD])
    below = (-1, with_swapped(below0, below1), NEAR)
    below_hi, below_lo, below_part = part_sizes(where, below, store)
    above = (1, with_swapped(above0, above1), NEAR)
    head, tail, below_part = tie(head, tail, below_part)
    across = (2, with_swapped(*far0, head, tail), FAR)
    rh, rl, *rest = ready_queries(
        where, [own, below, above, across], [(own_hi, own_lo), (below_hi, below_lo), (), ()]
    )

    up1, down1, up2, down2, mine = raw_scores(rh, rl, store, 0, SPLIT[0], Z_FIRST)
    rh = tie(rh, mine)[0]
    away, home = raw_scores(rh, rl, store, SPLIT[0], SPLIT[1], X_FIRST)
    rest_part = rest_sizes(where, [1, 2], tie(*rest, home)[:-1], store)
    from_below, from_above = z_up(up1), z_down(down1)
    came = swap_x(away)
    sizes_sq = own_part + below_part + rest_part
    sizes_sq, from_below, from_above = tie(sizes_sq, from_below, from_above)
    last_below, last_above = z_up(up2 + from_below[:32]), z_down(down2 + from_above[:32])
    sizes_sq = sizes_sq + swap_x(sizes_sq)
    home = home + came
    sizes_sq = sizes_sq + layer_permute(sizes_sq, lambda x_lo, z: (x_lo, z ^ 1))
    sizes_sq, last_below, last_above = tie(sizes_sq, last_below, last_above)
    here = mine[:32] + from_above[32:] + last_below
    there = mine[32:] + from_below[32:] + last_above
    first = here + swap_x(there)

    from_below, from_above = tie(z_up(home[:32]), z_down(home[32:64]))
    last_below = z_up(home[64:80] + from_below[:16])
    last_above = z_down(home[80:96] + from_above[:16])
    last = jnp.concatenate(
        [home[96:112] + from_above[16:] + last_below, home[112:] + from_below[16:] + last_above], axis=0
    )

    root = jnp.sqrt(sizes_sq + layer_permute(sizes_sq, lambda x_lo, z: (x_lo, z ^ 2)))
    return jnp.concatenate([first, last], axis=1) / root


def solution(mesh):
    in_specs = (
        P("layer", "example", None),
        P("layer", "example", None),
        P("layer", "example", None),
    )
    out_specs = P("layer", "example")
    return jax.shard_map(shards, mesh=mesh, in_specs=in_specs, out_specs=out_specs, check_vma=False)
```

```python
import functools

import jax
import jax.numpy as jnp
from jax import lax
from jax.experimental import pallas as pl
from jax.experimental.pallas import tpu as pltpu
from jax.sharding import PartitionSpec as P

R = 1024
Q = 256
ROWS = 64
QROWS = 16
PIECE = ROWS + QROWS
TILE = 2048
SPLIT = (2560, 1536)
BF16 = jnp.bfloat16
F32 = jnp.float32
LIMIT = 20 * 2**20
nt_dot = functools.partial(
    lax.dot_general, dimension_numbers=(((1,), (1,)), ((), ())), preferred_element_type=F32
)
VMEM = pl.BlockSpec(memory_space=pltpu.VMEM)
SMEM = pl.BlockSpec(memory_space=pltpu.SMEM)


def example_permute(x, to):
    pairs = []
    for x_hi in range(2):
        for y in range(4):
            for core in range(2):
                a, b, c = to(x_hi, y, core)
                pairs.append((x_hi * 8 + y * 2 + core, a * 8 + (b % 4) * 2 + c))
    return lax.ppermute(x, "example", pairs)


def layer_permute(x, to):
    pairs = []
    for x_lo in range(2):
        for z in range(4):
            a, b = to(x_lo, z)
            pairs.append((x_lo * 4 + z, a * 4 + b % 4))
    return lax.ppermute(x, "layer", pairs)


def y_up(x):
    return example_permute(x, lambda x_hi, y, core: (x_hi, y + 1, core))


def y_down(x):
    return example_permute(x, lambda x_hi, y, core: (x_hi, y - 1, core))


def with_swapped(*arrays):
    return list(arrays) + [example_permute(x, lambda x_hi, y, core: (x_hi, y, 1 - core)) for x in arrays]


def z_up(x):
    return layer_permute(x, lambda x_lo, z: (x_lo, z + 1))


def z_down(x):
    return layer_permute(x, lambda x_lo, z: (x_lo, z - 1))


def swap_x(x):
    return layer_permute(x, lambda x_lo, z: (1 - x_lo, z))


HEAD = 32
NEAR = [(0, 0, ROWS, ROWS, 0, 0), (1, 0, ROWS, ROWS, 1, 0), (2, 0, ROWS, ROWS, 0, 1), (3, 0, ROWS, ROWS, 1, 1)]
FAR = [
    (4 * core + 2 * x_flip + tail, HEAD * tail, HEAD, HEAD if tail else -1, x_flip, core)
    for core in range(2)
    for x_flip in range(2)
    for tail in range(2)
]


def tie(*arrays):
    return lax.optimization_barrier(arrays)


def split(blocks, bufs, x_hi, core, hi_ref, lo_ref):
    for b, first, n, _, x_flip, core_flip in blocks:
        at = ((x_hi + x_flip) % 2) * 2 + (core + core_flip) % 2
        rows = pl.ds(pl.multiple_of(at * ROWS + first, HEAD), n)
        block = bufs[b][:n, :]
        hi = block.astype(BF16)
        hi_ref[rows, :] = hi
        lo_ref[rows, :] = (block - hi.astype(F32)).astype(BF16)


def add_sizes(y_shifts, y, s_ref, matrices, o_ref):
    @pl.loop(0, o_ref.shape[1] // TILE)
    def _(i):
        rows = pl.ds(pl.multiple_of(i * TILE, TILE), TILE)
        sh = s_ref[rows, :].astype(BF16)
        total = 0.0
        for y_shift, (hi_ref, lo_ref) in zip(y_shifts, matrices):
            moved = nt_dot(sh, hi_ref[...]) + nt_dot(sh, lo_ref[...])
            first = pl.multiple_of(((y + y_shift + 4) % 4) * 128, 128)
            for half in range(2):
                cols = pl.ds(first + half * 512, 128)
                own = s_ref[rows, cols]
                weight = 2.0 * own - own.astype(BF16).astype(F32)
                total += moved[:, half * 128 : half * 128 + 128] * weight
        o_ref[:, rows] = jnp.sum(total.T, axis=0, keepdims=True)


def part_kernel(blocks, y_shift, n, where_ref, *refs):
    bufs, (s_ref, hi_ref, lo_ref, o_ref) = refs[:n], refs[n:]
    me = where_ref[0]
    split(blocks, bufs, me // 8, me % 2, hi_ref, lo_ref)
    add_sizes([y_shift], (me // 2) % 4, s_ref, [(hi_ref, lo_ref)], o_ref)


def part_sizes(where, part, store):
    y_shift, buffers, blocks = part
    examples = store.shape[0]
    return pl.pallas_call(
        functools.partial(part_kernel, blocks, y_shift, len(buffers)),
        in_specs=[SMEM] + [VMEM] * (len(buffers) + 1),
        out_specs=[VMEM] * 3,
        out_shape=[jax.ShapeDtypeStruct((256, R), BF16)] * 2 + [jax.ShapeDtypeStruct((1, examples), F32)],
        compiler_params=pltpu.CompilerParams(vmem_limit_bytes=LIMIT),
        cost_estimate=pl.CostEstimate(
            flops=8 * 256 * R * examples, bytes_accessed=4 * R * examples, transcendentals=0
        ),
    )(where, *buffers, store)


def rest_kernel(y_shifts, where_ref, *refs):
    mats, (s_ref, o_ref) = refs[:-2], refs[-2:]
    pairs = [(mats[2 * k], mats[2 * k + 1]) for k in range(len(y_shifts))]
    add_sizes(y_shifts, (where_ref[0] // 2) % 4, s_ref, pairs, o_ref)


def rest_sizes(where, y_shifts, matrices, store):
    examples = store.shape[0]
    return pl.pallas_call(
        functools.partial(rest_kernel, y_shifts),
        in_specs=[SMEM] + [VMEM] * (len(matrices) + 1),
        out_specs=VMEM,
        out_shape=jax.ShapeDtypeStruct((1, examples), F32),
        compiler_params=pltpu.CompilerParams(vmem_limit_bytes=LIMIT),
        cost_estimate=pl.CostEstimate(flops=1, bytes_accessed=1, transcendentals=0),
    )(where, *matrices, store)


SLOTS = (6, 7, 4, 1, 0, 2, 3, 5)


def ready_kernel(parts, n, where_ref, *refs):
    ins, (rh_ref, rl_ref, *made), q_ref = refs[:n], refs[n:-1], refs[-1]
    me, x_lo, z = where_ref[0], where_ref[1], where_ref[2]
    x_hi, y, core = me // 8, (me // 2) % 4, me % 2
    matrices = []
    for y_shift, first, count, blocks, ready_made in parts:
        bufs = ins[first : first + count]
        if ready_made:
            matrices.append((y_shift, ins[first + count], ins[first + count + 1]))
        else:
            hi_ref, lo_ref, *made = made
            split(blocks, bufs, x_hi, core, hi_ref, lo_ref)
            matrices.append((y_shift, hi_ref, lo_ref))
        for b, _, _, queries, x_flip, core_flip in blocks:
            if queries < 0:
                continue
            to_z, to_x = (y + y_shift + 4) % 4, (x_hi + x_flip) % 2
            code = ((to_z - z + 4) % 4) * 2 + (to_x + x_lo) % 2
            slot = sum(jnp.where(code == k, s, 0) for k, s in enumerate(SLOTS))
            at = slot * 2 + (core + core_flip) % 2
            rows = pl.ds(pl.multiple_of(at * QROWS, QROWS), QROWS)
            q_ref[rows, :] = bufs[b][queries : queries + QROWS, :]
    q = q_ref[...]
    qh = q.astype(BF16)
    ql = (q - qh.astype(F32)).astype(BF16)
    for y_shift, hi_ref, lo_ref in matrices:
        ready = nt_dot(qh, hi_ref[...]) + nt_dot(qh, lo_ref[...]) + nt_dot(ql, hi_ref[...])
        high = ready.astype(BF16)
        low = (ready - high.astype(F32)).astype(BF16)
        start = pl.multiple_of(((y + y_shift + 4) % 4) * 128, 128)
        for half in range(2):
            cols = pl.ds(start + half * 512, 128)
            rh_ref[:, cols] = high[:, half * 128 : half * 128 + 128]
            rl_ref[:, cols] = low[:, half * 128 : half * 128 + 128]


def ready_queries(where, parts, matrices):
    refs, rows, missing = [], [], 0
    for (y_shift, buffers, blocks), made in zip(parts, matrices):
        rows.append((y_shift, len(refs), len(buffers), blocks, bool(made)))
        refs += list(buffers) + list(made)
        missing += not made
    shapes = [(Q, R)] * 2 + [(256, R)] * (2 * missing)
    return pl.pallas_call(
        functools.partial(ready_kernel, rows, len(refs)),
        in_specs=[SMEM] + [VMEM] * len(refs),
        out_specs=[VMEM] * len(shapes),
        out_shape=[jax.ShapeDtypeStruct(shape, BF16) for shape in shapes],
        scratch_shapes=[pltpu.VMEM((Q, R), F32)],
        compiler_params=pltpu.CompilerParams(vmem_limit_bytes=LIMIT),
        cost_estimate=pl.CostEstimate(flops=6 * Q * R * R, bytes_accessed=2**20, transcendentals=0),
    )(where, *refs)


Z_FIRST = [[(0, 64)], [(64, 64)], [(128, 32)], [(160, 32)], [(192, 64)]]
HALVES = ((2, 0), (1, 1), (2, 1), (3, 0), (1, 0), (3, 1), (0, 0), (0, 1))
X_FIRST = [[(32 * SLOTS[2 * dz + dx] + 16 * half, 16) for dz, half in HALVES] for dx in (1, 0)]


def raw_kernel(first, runs, rh_ref, rl_ref, s_ref, *outs):
    size = outs[0].shape[1] // 2

    @pl.loop(0, 2)
    def _(i):
        rows = pl.ds(pl.multiple_of(first + i * size, size), size)
        cols = pl.ds(pl.multiple_of(i * size, size), size)
        s = s_ref[rows, :]
        sh = s.astype(BF16)
        sl = (s - sh.astype(F32)).astype(BF16)
        raw = nt_dot(rh_ref[...], sh) + nt_dot(rh_ref[...], sl) + nt_dot(rl_ref[...], sh)
        for run, ref in zip(runs, outs):
            at = 0
            for start, n in run:
                ref[at : at + n, cols] = raw[start : start + n]
                at += n


def raw_scores(rh, rl, store, first, examples, runs):
    return pl.pallas_call(
        functools.partial(raw_kernel, first, runs),
        in_specs=[VMEM] * 3,
        out_specs=[VMEM] * len(runs),
        out_shape=[jax.ShapeDtypeStruct((sum(n for _, n in run), examples), F32) for run in runs],
        compiler_params=pltpu.CompilerParams(vmem_limit_bytes=LIMIT),
        cost_estimate=pl.CostEstimate(
            flops=8 * Q * R * examples, bytes_accessed=4 * (R + Q) * examples, transcendentals=0
        ),
    )(rh, rl, store)


def shards(queries, precond, store):
    layer = lax.axis_index("layer")
    where = jnp.stack([lax.axis_index("example"), layer // 4, layer % 4]).astype(jnp.int32)
    store = store[0]

    own0 = jnp.concatenate([precond[0], queries[0]], axis=0)
    own1 = example_permute(own0, lambda x_hi, y, core: (1 - x_hi, y, core))
    own1, below0, above0 = tie(own1, y_up(own0), y_down(own0))
    own = (0, with_swapped(own0, own1), NEAR)
    own_hi, own_lo, own_part = part_sizes(where, own, store)
    below1, above1, *far0, own_part = tie(
        y_up(own1), y_down(own1), y_up(below0[:HEAD]), y_down(above0[HEAD:]), own_part
    )
    tail, head = y_up(below1[HEAD:]), y_down(above1[:HEAD])
    below = (-1, with_swapped(below0, below1), NEAR)
    below_hi, below_lo, below_part = part_sizes(where, below, store)
    above = (1, with_swapped(above0, above1), NEAR)
    head, tail, below_part = tie(head, tail, below_part)
    across = (2, with_swapped(*far0, head, tail), FAR)
    rh, rl, *rest = ready_queries(
        where, [own, below, above, across], [(own_hi, own_lo), (below_hi, below_lo), (), ()]
    )

    up1, down1, up2, down2, mine = raw_scores(rh, rl, store, 0, SPLIT[0], Z_FIRST)
    rh = tie(rh, mine)[0]
    away, home = raw_scores(rh, rl, store, SPLIT[0], SPLIT[1], X_FIRST)
    rest_part = rest_sizes(where, [1, 2], tie(*rest, home)[:-1], store)
    from_below, from_above = z_up(up1), z_down(down1)
    came = swap_x(away)
    sizes_sq = own_part + below_part + rest_part
    sizes_sq, from_below, from_above = tie(sizes_sq, from_below, from_above)
    last_below, last_above = z_up(up2 + from_below[:32]), z_down(down2 + from_above[:32])
    sizes_sq = sizes_sq + swap_x(sizes_sq)
    home = home + came
    sizes_sq = sizes_sq + layer_permute(sizes_sq, lambda x_lo, z: (x_lo, z ^ 2))
    sizes_sq, last_below, last_above = tie(sizes_sq, last_below, last_above)
    here = mine[:32] + from_above[32:] + last_below
    there = mine[32:] + from_below[32:] + last_above
    first = here + swap_x(there)

    from_below, from_above = tie(z_up(home[:32]), z_down(home[32:64]))
    last_below = z_up(home[64:80] + from_below[:16])
    last_above = z_down(home[80:96] + from_above[:16])
    last = jnp.concatenate(
        [home[96:112] + from_above[16:] + last_below, home[112:] + from_below[16:] + last_above], axis=0
    )

    root = jnp.sqrt(sizes_sq + layer_permute(sizes_sq, lambda x_lo, z: (x_lo, z ^ 1)))
    return jnp.concatenate([first, last], axis=1) / root


def solution(mesh):
    in_specs = (
        P("layer", "example", None),
        P("layer", "example", None),
        P("layer", "example", None),
    )
    out_specs = P("layer", "example")
    return jax.shard_map(shards, mesh=mesh, in_specs=in_specs, out_specs=out_specs, check_vma=False)
```

```python
import functools

import jax
import jax.numpy as jnp
from jax import lax
from jax.experimental import pallas as pl
from jax.experimental.pallas import tpu as pltpu
from jax.sharding import PartitionSpec as P

R = 1024
Q = 256
ROWS = 64
QROWS = 16
PIECE = ROWS + QROWS
TILE = 2048
SPLIT = (2560, 1536)
BF16 = jnp.bfloat16
F32 = jnp.float32
LIMIT = 20 * 2**20
nt_dot = functools.partial(
    lax.dot_general, dimension_numbers=(((1,), (1,)), ((), ())), preferred_element_type=F32
)
VMEM = pl.BlockSpec(memory_space=pltpu.VMEM)
SMEM = pl.BlockSpec(memory_space=pltpu.SMEM)


def example_permute(x, to):
    pairs = []
    for x_hi in range(2):
        for y in range(4):
            for core in range(2):
                a, b, c = to(x_hi, y, core)
                pairs.append((x_hi * 8 + y * 2 + core, a * 8 + (b % 4) * 2 + c))
    return lax.ppermute(x, "example", pairs)


def layer_permute(x, to):
    pairs = []
    for x_lo in range(2):
        for z in range(4):
            a, b = to(x_lo, z)
            pairs.append((x_lo * 4 + z, a * 4 + b % 4))
    return lax.ppermute(x, "layer", pairs)


def swap_x_hi(x):
    return example_permute(x, lambda x_hi, y, core: (1 - x_hi, y, core))


def y_up(x):
    return example_permute(x, lambda x_hi, y, core: (x_hi, y + 1, core))


def y_down(x):
    return example_permute(x, lambda x_hi, y, core: (x_hi, y - 1, core))


def with_swapped(*arrays):
    return list(arrays) + [example_permute(x, lambda x_hi, y, core: (x_hi, y, 1 - core)) for x in arrays]


def z_up(x):
    return layer_permute(x, lambda x_lo, z: (x_lo, z + 1))


def z_down(x):
    return layer_permute(x, lambda x_lo, z: (x_lo, z - 1))


def swap_x(x):
    return layer_permute(x, lambda x_lo, z: (1 - x_lo, z))


HEAD = 32
NEAR = [(0, 0, ROWS, ROWS, 0, 0), (1, 0, ROWS, ROWS, 1, 0), (2, 0, ROWS, ROWS, 0, 1), (3, 0, ROWS, ROWS, 1, 1)]
FAR = [
    block
    for core in range(2)
    for block in (
        (3 * core, 0, ROWS, ROWS, 0, core),
        (3 * core + 1, 0, HEAD, -1, 1, core),
        (3 * core + 2, HEAD, HEAD, HEAD, 1, core),
    )
]


def tie(*arrays):
    return lax.optimization_barrier(arrays)


def split(blocks, bufs, x_hi, core, hi_ref, lo_ref):
    for b, first, n, _, x_flip, core_flip in blocks:
        at = ((x_hi + x_flip) % 2) * 2 + (core + core_flip) % 2
        rows = pl.ds(pl.multiple_of(at * ROWS + first, HEAD), n)
        block = bufs[b][:n, :]
        hi = block.astype(BF16)
        hi_ref[rows, :] = hi
        lo_ref[rows, :] = (block - hi.astype(F32)).astype(BF16)


def add_sizes(y_shifts, y, s_ref, matrices, o_ref):
    @pl.loop(0, o_ref.shape[1] // TILE)
    def _(i):
        rows = pl.ds(pl.multiple_of(i * TILE, TILE), TILE)
        sh = s_ref[rows, :].astype(BF16)
        total = 0.0
        for y_shift, (hi_ref, lo_ref) in zip(y_shifts, matrices):
            moved = nt_dot(sh, hi_ref[...]) + nt_dot(sh, lo_ref[...])
            first = pl.multiple_of(((y + y_shift + 4) % 4) * 128, 128)
            for half in range(2):
                cols = pl.ds(first + half * 512, 128)
                own = s_ref[rows, cols]
                weight = 2.0 * own - own.astype(BF16).astype(F32)
                total += moved[:, half * 128 : half * 128 + 128] * weight
        o_ref[:, rows] = jnp.sum(total.T, axis=0, keepdims=True)


def part_kernel(blocks, y_shift, n, where_ref, *refs):
    bufs, (s_ref, hi_ref, lo_ref, o_ref) = refs[:n], refs[n:]
    me = where_ref[0]
    split(blocks, bufs, me // 8, me % 2, hi_ref, lo_ref)
    add_sizes([y_shift], (me // 2) % 4, s_ref, [(hi_ref, lo_ref)], o_ref)


def part_sizes(where, part, store):
    y_shift, buffers, blocks = part
    examples = store.shape[0]
    return pl.pallas_call(
        functools.partial(part_kernel, blocks, y_shift, len(buffers)),
        in_specs=[SMEM] + [VMEM] * (len(buffers) + 1),
        out_specs=[VMEM] * 3,
        out_shape=[jax.ShapeDtypeStruct((256, R), BF16)] * 2 + [jax.ShapeDtypeStruct((1, examples), F32)],
        compiler_params=pltpu.CompilerParams(vmem_limit_bytes=LIMIT),
        cost_estimate=pl.CostEstimate(
            flops=8 * 256 * R * examples, bytes_accessed=4 * R * examples, transcendentals=0
        ),
    )(where, *buffers, store)


def rest_kernel(y_shifts, where_ref, *refs):
    mats, (s_ref, o_ref) = refs[:-2], refs[-2:]
    pairs = [(mats[2 * k], mats[2 * k + 1]) for k in range(len(y_shifts))]
    add_sizes(y_shifts, (where_ref[0] // 2) % 4, s_ref, pairs, o_ref)


def rest_sizes(where, y_shifts, matrices, store):
    examples = store.shape[0]
    return pl.pallas_call(
        functools.partial(rest_kernel, y_shifts),
        in_specs=[SMEM] + [VMEM] * (len(matrices) + 1),
        out_specs=VMEM,
        out_shape=jax.ShapeDtypeStruct((1, examples), F32),
        compiler_params=pltpu.CompilerParams(vmem_limit_bytes=LIMIT),
        cost_estimate=pl.CostEstimate(flops=1, bytes_accessed=1, transcendentals=0),
    )(where, *matrices, store)


SLOTS = (6, 7, 4, 1, 0, 2, 3, 5)


def ready_kernel(parts, n, where_ref, *refs):
    ins, (rh_ref, rl_ref, *made), q_ref = refs[:n], refs[n:-1], refs[-1]
    me, x_lo, z = where_ref[0], where_ref[1], where_ref[2]
    x_hi, y, core = me // 8, (me // 2) % 4, me % 2
    matrices = []
    for y_shift, first, count, blocks, ready_made in parts:
        bufs = ins[first : first + count]
        if ready_made:
            matrices.append((y_shift, ins[first + count], ins[first + count + 1]))
        else:
            hi_ref, lo_ref, *made = made
            split(blocks, bufs, x_hi, core, hi_ref, lo_ref)
            matrices.append((y_shift, hi_ref, lo_ref))
        for b, _, _, queries, x_flip, core_flip in blocks:
            if queries < 0:
                continue
            to_z, to_x = (y + y_shift + 4) % 4, (x_hi + x_flip) % 2
            code = ((to_z - z + 4) % 4) * 2 + (to_x + x_lo) % 2
            slot = sum(jnp.where(code == k, s, 0) for k, s in enumerate(SLOTS))
            at = slot * 2 + (core + core_flip) % 2
            rows = pl.ds(pl.multiple_of(at * QROWS, QROWS), QROWS)
            q_ref[rows, :] = bufs[b][queries : queries + QROWS, :]
    q = q_ref[...]
    qh = q.astype(BF16)
    ql = (q - qh.astype(F32)).astype(BF16)
    for y_shift, hi_ref, lo_ref in matrices:
        ready = nt_dot(qh, hi_ref[...]) + nt_dot(qh, lo_ref[...]) + nt_dot(ql, hi_ref[...])
        high = ready.astype(BF16)
        low = (ready - high.astype(F32)).astype(BF16)
        start = pl.multiple_of(((y + y_shift + 4) % 4) * 128, 128)
        for half in range(2):
            cols = pl.ds(start + half * 512, 128)
            rh_ref[:, cols] = high[:, half * 128 : half * 128 + 128]
            rl_ref[:, cols] = low[:, half * 128 : half * 128 + 128]


def ready_queries(where, parts, matrices):
    refs, rows, missing = [], [], 0
    for (y_shift, buffers, blocks), made in zip(parts, matrices):
        rows.append((y_shift, len(refs), len(buffers), blocks, bool(made)))
        refs += list(buffers) + list(made)
        missing += not made
    shapes = [(Q, R)] * 2 + [(256, R)] * (2 * missing)
    return pl.pallas_call(
        functools.partial(ready_kernel, rows, len(refs)),
        in_specs=[SMEM] + [VMEM] * len(refs),
        out_specs=[VMEM] * len(shapes),
        out_shape=[jax.ShapeDtypeStruct(shape, BF16) for shape in shapes],
        scratch_shapes=[pltpu.VMEM((Q, R), F32)],
        compiler_params=pltpu.CompilerParams(vmem_limit_bytes=LIMIT),
        cost_estimate=pl.CostEstimate(flops=6 * Q * R * R, bytes_accessed=2**20, transcendentals=0),
    )(where, *refs)


Z_FIRST = [[(0, 64)], [(64, 64)], [(128, 32)], [(160, 32)], [(192, 64)]]
HALVES = ((2, 0), (1, 1), (2, 1), (3, 0), (1, 0), (3, 1), (0, 0), (0, 1))
X_FIRST = [[(32 * SLOTS[2 * dz + dx] + 16 * half, 16) for dz, half in HALVES] for dx in (1, 0)]


def raw_kernel(first, runs, rh_ref, rl_ref, s_ref, *outs):
    size = outs[0].shape[1] // 2

    @pl.loop(0, 2)
    def _(i):
        rows = pl.ds(pl.multiple_of(first + i * size, size), size)
        cols = pl.ds(pl.multiple_of(i * size, size), size)
        s = s_ref[rows, :]
        sh = s.astype(BF16)
        sl = (s - sh.astype(F32)).astype(BF16)
        raw = nt_dot(rh_ref[...], sh) + nt_dot(rh_ref[...], sl) + nt_dot(rl_ref[...], sh)
        for run, ref in zip(runs, outs):
            at = 0
            for start, n in run:
                ref[at : at + n, cols] = raw[start : start + n]
                at += n


def raw_scores(rh, rl, store, first, examples, runs):
    return pl.pallas_call(
        functools.partial(raw_kernel, first, runs),
        in_specs=[VMEM] * 3,
        out_specs=[VMEM] * len(runs),
        out_shape=[jax.ShapeDtypeStruct((sum(n for _, n in run), examples), F32) for run in runs],
        compiler_params=pltpu.CompilerParams(vmem_limit_bytes=LIMIT),
        cost_estimate=pl.CostEstimate(
            flops=8 * Q * R * examples, bytes_accessed=4 * (R + Q) * examples, transcendentals=0
        ),
    )(rh, rl, store)


def shards(queries, precond, store):
    layer = lax.axis_index("layer")
    where = jnp.stack([lax.axis_index("example"), layer // 4, layer % 4]).astype(jnp.int32)
    store = store[0]

    own0 = jnp.concatenate([precond[0], queries[0]], axis=0)
    own1 = swap_x_hi(own0)
    own1, below0, above0 = tie(own1, y_up(own0), y_down(own0))
    own = (0, with_swapped(own0, own1), NEAR)
    own_hi, own_lo, own_part = part_sizes(where, own, store)
    below1, above1, far0, own_part = tie(swap_x_hi(below0), y_down(own1), y_up(below0), own_part)
    tail, head = y_up(below1[HEAD:]), y_down(above1[:HEAD])
    below = (-1, with_swapped(below0, below1), NEAR)
    below_hi, below_lo, below_part = part_sizes(where, below, store)
    above = (1, with_swapped(above0, above1), NEAR)
    head, tail, below_part = tie(head, tail, below_part)
    across = (2, with_swapped(far0, head, tail), FAR)
    rh, rl, *rest = ready_queries(
        where, [own, below, above, across], [(own_hi, own_lo), (below_hi, below_lo), (), ()]
    )

    up1, down1, up2, down2, mine = raw_scores(rh, rl, store, 0, SPLIT[0], Z_FIRST)
    rh = tie(rh, mine)[0]
    away, home = raw_scores(rh, rl, store, SPLIT[0], SPLIT[1], X_FIRST)
    rest_part = rest_sizes(where, [1, 2], tie(*rest, home)[:-1], store)
    from_below, from_above = z_up(up1), z_down(down1)
    came = swap_x(away)
    sizes_sq = own_part + below_part + rest_part
    sizes_sq, from_below, from_above = tie(sizes_sq, from_below, from_above)
    last_below, last_above = z_up(up2 + from_below[:32]), z_down(down2 + from_above[:32])
    sizes_sq = sizes_sq + swap_x(sizes_sq)
    home = home + came
    sizes_sq, last_below, last_above = tie(sizes_sq, last_below, last_above)
    sizes_sq = sizes_sq + layer_permute(sizes_sq, lambda x_lo, z: (x_lo, z ^ 1))
    here = mine[:32] + from_above[32:] + last_below
    there = mine[32:] + from_below[32:] + last_above
    first = here + swap_x(there)

    from_below, from_above = tie(z_up(home[:32]), z_down(home[32:64]))
    last_below = z_up(home[64:80] + from_below[:16])
    last_above = z_down(home[80:96] + from_above[:16])
    last = jnp.concatenate(
        [home[96:112] + from_above[16:] + last_below, home[112:] + from_below[16:] + last_above], axis=0
    )

    root = jnp.sqrt(sizes_sq + layer_permute(sizes_sq, lambda x_lo, z: (x_lo, z ^ 2)))
    return jnp.concatenate([first, last], axis=1) / root


def solution(mesh):
    in_specs = (
        P("layer", "example", None),
        P("layer", "example", None),
        P("layer", "example", None),
    )
    out_specs = P("layer", "example")
    return jax.shard_map(shards, mesh=mesh, in_specs=in_specs, out_specs=out_specs, check_vma=False)
```
